32 devices in a mesh: groups: 2 (over y), seq: 4 (over z), head: 2 (over x), pair: 2 (over core).
Axes of the slice: x: 2, y: 2, z: 4, core: 2. Of those that a mesh axis runs over, the one named last changes fastest.
Arguments:
- queries: bfloat16 [8192, 40, 128], P(('groups', 'seq'), ('head', 'pair')), parts along dimension 0, may hold values from -4 to 4
- keys: bfloat16 [8192, 40, 128], P(('groups', 'seq'), ('head', 'pair')), parts along dimension 0, may hold values from -4 to 4
- values: bfloat16 [8192, 40, 128], P(('groups', 'seq'), ('head', 'pair')), parts along dimension 0, may hold values from -4 to 4
- grad_out: bfloat16 [8192, 40, 128], P(('groups', 'seq'), ('head', 'pair')), parts along dimension 0, may hold values from -5 to 5
- fine_out: bfloat16 [8192, 40, 128], P(('groups', 'seq'), ('head', 'pair')), parts along dimension 0, may hold values from -5 to 5
- coarse_out: bfloat16 [8192, 40, 128], P(('groups', 'seq'), ('head', 'pair')), parts along dimension 0, may hold values from -5 to 5
- fine_lse: float32 [40, 8192], P(('head', 'pair'), ('groups', 'seq')), parts along dimension 1, may hold values from 6.5 to 8.5
- coarse_lse: float32 [40, 8192], P(('head', 'pair'), ('groups', 'seq')), parts along dimension 1, may hold values from 5 to 7
- select: int32 [128, 1], P(('groups', 'seq')), parts along dimension 0, may hold values from 0 to 63, as said below
Outputs:
- grad_queries: bfloat16 [8192, 40, 128], P(('groups', 'seq'), ('head', 'pair')), parts along dimension 0
- grad_keys: bfloat16 [8192, 40, 128], P(('groups', 'seq'), ('head', 'pair')), parts along dimension 0
- grad_values: bfloat16 [8192, 40, 128], P(('groups', 'seq'), ('head', 'pair')), parts along dimension 0
- pooled_key_grad: float32 [128, 40, 128], P(('groups', 'seq'), ('head', 'pair')), parts along dimension 0
- pooled_value_grad: float32 [128, 40, 128], P(('groups', 'seq'), ('head', 'pair')), parts along dimension 0
The draws below stay inside these ranges and needn't reach their ends.
There are 2 independent parts, one for each index of `groups`. The reference program is written for one: setup_inputs(seed, part) draws one part's arguments, and reference() takes and returns one part's arrays. A program takes and returns all parts, laid end to end along the dimension named above; each array names one. Nothing has to cross between parts.
Inputs may be any that keep to these rules, and one draw needn't show every extreme that they name: `select`: each entry names a cube outside the query cube's own aligned group of 16 cubes; a query cube's 1 entries are distinct. The query cubes of one aligned group name at most 8 cubes of any one other group, counted with repeats; in every draw 1 group are named exactly 8 times by every other group.
All inputs are finite; a program needn't handle non-finite values.
Results may differ from the reference program's by a relative error of at most 0.017.
Values may be sent and summed in bfloat16 or wider, within the bound.
A program may use at most 256 MiB of HBM per device.

```python
import jax
import jax.numpy as jnp
from jax import lax

HEADS = 40
HEAD_DIM = 128
CUBE = 64
CUBES_DEV = 16
FAR = 1
NC = 64
TOKENS = 4096
HOT = 1
CAP = 8
N_SEQ = 4


def draw_keys(key, part):
    key = jax.random.fold_in(key, 3)
    first, second = jax.random.split(key)
    common = jax.random.normal(first, (NC, 1, HEADS, HEAD_DIM), jnp.float32)
    detail = jax.random.normal(second, (NC, CUBE, HEADS, HEAD_DIM), jnp.float32)
    field = jnp.clip(0.8 * common + 0.6 * detail, -4.0, 4.0)
    return field.reshape(TOKENS, HEADS, HEAD_DIM).astype(jnp.bfloat16)


def draw_values(key, part):
    key = jax.random.fold_in(key, 5)
    first, second = jax.random.split(key)
    common = jax.random.normal(first, (NC, 1, HEADS, HEAD_DIM), jnp.float32)
    detail = jax.random.normal(second, (NC, CUBE, HEADS, HEAD_DIM), jnp.float32)
    field = jnp.clip(0.8 * common + 0.6 * detail, -4.0, 4.0)
    return field.reshape(TOKENS, HEADS, HEAD_DIM).astype(jnp.bfloat16)


def draw_select(key, part):
    key = jax.random.fold_in(key, 7)
    hot_key, slot_key, order_key, cube_key = jax.random.split(key, 4)
    task_total = CUBES_DEV * FAR
    peers = jnp.arange(N_SEQ, dtype=jnp.int32)
    hot_rank = jax.random.permutation(hot_key, N_SEQ)
    is_hot = hot_rank < HOT
    slot_peer = jnp.arange(N_SEQ * CAP, dtype=jnp.int32) // CAP

    def sender(sender_index, shuffle_key, task_key):
        hot_other = is_hot & (peers != sender_index)
        cold_slot = jnp.logical_not(is_hot[slot_peer]) & (slot_peer != sender_index)
        remaining = task_total - CAP * jnp.sum(hot_other.astype(jnp.int32))
        ranking = jax.random.permutation(shuffle_key, N_SEQ * CAP)
        before = jnp.sum((cold_slot[None, :] & (ranking[None, :] < ranking[:, None])).astype(jnp.int32), axis=1)
        chosen = cold_slot & (before < remaining)
        counts = CAP * hot_other.astype(jnp.int32) + jnp.sum(((slot_peer[None, :] == peers[:, None]) & chosen[None, :]).astype(jnp.int32), axis=1)
        ends = jnp.cumsum(counts)
        positions = jnp.arange(task_total, dtype=jnp.int32)
        target = jnp.sum((ends[None, :] <= positions[:, None]).astype(jnp.int32), axis=1)
        return jax.random.permutation(task_key, target)
    senders = jnp.arange(N_SEQ, dtype=jnp.int32)
    targets = jax.vmap(sender)(senders, jax.random.split(slot_key, N_SEQ), jax.random.split(order_key, N_SEQ))
    local_cube = jax.vmap(lambda k: jax.random.permutation(k, CUBES_DEV)[:FAR])(jax.random.split(cube_key, NC))
    devices = targets.reshape(NC, FAR)
    return (devices * CUBES_DEV + local_cube).astype(jnp.int32)


def shard_levels(own_key, extent, cuts, least, high):
    def one(axis_at, parts):
        draws = jax.random.uniform(jax.random.fold_in(jax.random.fold_in(own_key, 6), axis_at), (parts,), jnp.float32, least / len(cuts), high / len(cuts))
        return jnp.repeat(jnp.exp(draws), extent[axis_at] // parts).reshape((-1,) + (1,) * (len(extent) - axis_at - 1))

    gain = one(*cuts[0])
    for cut in cuts[1:]:
        gain = gain * one(*cut)
    return gain


def gaussian(own_key, extent, scale, bound, cuts=(), kind=jnp.bfloat16):
    values = jax.random.normal(own_key, extent, jnp.float32) * scale
    if len(cuts) > 0:
        values = shard_levels(own_key, extent, cuts, -0.22, 0.18) * values
    return jnp.clip(values, min=-bound, max=bound).astype(kind)


def setup_inputs(seed: int = 0, part: int = 0) -> dict:
    key_of = jax.random.split(jax.random.key(seed), 10)
    own_keys = jax.random.split(jax.random.fold_in(key_of[9], part), 10)
    return {
        "queries": gaussian(own_keys[0], (TOKENS, HEADS, HEAD_DIM), 1.0, 4.0, ((0, 4), (1, 4))),
        "keys": draw_keys(jax.random.fold_in(jax.random.fold_in(key_of[9], part), 71), part),
        "values": draw_values(jax.random.fold_in(jax.random.fold_in(key_of[9], part), 71), part),
        "grad_out": gaussian(own_keys[3], (TOKENS, HEADS, HEAD_DIM), 1.0, 5.0, ((0, 4), (1, 4))),
        "fine_out": gaussian(own_keys[4], (TOKENS, HEADS, HEAD_DIM), 1.0, 5.0, ((0, 4), (1, 4))),
        "coarse_out": gaussian(own_keys[5], (TOKENS, HEADS, HEAD_DIM), 1.0, 5.0, ((0, 4), (1, 4))),
        "fine_lse": jnp.clip(6.5 + 2.0 * jax.random.uniform(own_keys[6], (HEADS, TOKENS), jnp.float32) ** shard_levels(own_keys[6], (HEADS, TOKENS), ((0, 4), (1, 4)), -0.2, 0.2), 6.5, 8.5),
        "coarse_lse": jnp.clip(5.0 + 2.0 * jax.random.uniform(own_keys[7], (HEADS, TOKENS), jnp.float32) ** shard_levels(own_keys[7], (HEADS, TOKENS), ((0, 4), (1, 4)), -0.2, 0.2), 5.0, 7.0),
        "select": draw_select(jax.random.fold_in(jax.random.fold_in(key_of[9], part), 71), part),
    }


def attend_grads(query_x, dout_x, lse_x, delta_x, key_x, value_x, scaling):
    query_f = query_x.astype(jnp.float32)
    dout_f = dout_x.astype(jnp.float32)
    key_f = key_x.astype(jnp.float32)
    value_f = value_x.astype(jnp.float32)
    scores = scaling * jnp.einsum('...qhe,...khe->...hqk', query_f, key_f)
    probs = jnp.exp(scores - lse_x[..., None])
    probs_low = lax.optimization_barrier(probs.astype(jnp.bfloat16)).astype(jnp.float32)
    dprobs = jnp.einsum('...qhe,...khe->...hqk', dout_f, value_f)
    dscores = (probs * (dprobs - delta_x[..., None])).astype(jnp.bfloat16)
    dscores = lax.optimization_barrier(dscores).astype(jnp.float32)
    grad_q = scaling * jnp.einsum('...hqk,...khe->...qhe', dscores, key_f)
    grad_k = scaling * jnp.einsum('...hqk,...qhe->...khe', dscores, query_f)
    grad_v = jnp.einsum('...hqk,...qhe->...khe', probs_low, dout_f)
    return grad_q, grad_k, grad_v


def reference(queries, keys, values, grad_out, fine_out, coarse_out, fine_lse, coarse_lse, select):
    scaling = HEAD_DIM ** -0.5
    group_rows = CUBES_DEV * CUBE
    dout_f = grad_out.astype(jnp.float32)
    delta_fine = jnp.einsum('the,the->ht', dout_f, fine_out.astype(jnp.float32))
    delta_coarse = jnp.einsum('the,the->ht', dout_f, coarse_out.astype(jnp.float32))

    def grouped(x):
        return x.reshape(N_SEQ, group_rows, HEADS, HEAD_DIM)

    def grouped_stat(x):
        return x.reshape(HEADS, N_SEQ, group_rows).transpose(1, 0, 2)

    def flatten(x):
        return x.reshape(TOKENS, HEADS, HEAD_DIM)

    def cubed(x):
        return x.reshape(NC, CUBE, HEADS, HEAD_DIM)

    def near_group(pieces):
        query_g, dout_g, key_g, value_g, lse_g, delta_g = pieces
        return attend_grads(query_g, dout_g, lse_g, delta_g, key_g, value_g, scaling)

    near_q, near_k, near_v = lax.map(near_group, (grouped(queries), grouped(grad_out), grouped(keys),
                                                  grouped(values), grouped_stat(fine_lse), grouped_stat(delta_fine)))

    query_cubes = cubed(queries)
    dout_cubes = cubed(grad_out)
    key_cubes = cubed(keys)
    value_cubes = cubed(values)
    lse_cubes = fine_lse.reshape(HEADS, NC, CUBE).transpose(1, 0, 2)
    delta_cubes = delta_fine.reshape(HEADS, NC, CUBE).transpose(1, 0, 2)
    sources = (jnp.arange(NC * FAR) // FAR).astype(jnp.int32)
    targets = select.reshape(-1).astype(jnp.int32)

    def far_block(pieces):
        source_b, target_b = pieces
        grads = attend_grads(query_cubes[source_b], dout_cubes[source_b], lse_cubes[source_b],
                             delta_cubes[source_b], key_cubes[target_b], value_cubes[target_b], scaling)
        return tuple(lax.optimization_barrier(g.astype(jnp.bfloat16)) for g in grads)

    task_q, task_k, task_v = lax.map(far_block, (sources.reshape(N_SEQ, -1), targets.reshape(N_SEQ, -1)))
    far_q = task_q.astype(jnp.float32).reshape(NC, FAR, CUBE, HEADS, HEAD_DIM).sum(axis=1)
    far_k = jax.ops.segment_sum(task_k.astype(jnp.float32).reshape(NC * FAR, CUBE, HEADS, HEAD_DIM), targets, num_segments=NC)
    far_v = jax.ops.segment_sum(task_v.astype(jnp.float32).reshape(NC * FAR, CUBE, HEADS, HEAD_DIM), targets, num_segments=NC)

    pooled_keys = key_cubes.astype(jnp.float32).mean(axis=1).astype(jnp.bfloat16)
    pooled_values = value_cubes.astype(jnp.float32).mean(axis=1).astype(jnp.bfloat16)

    def coarse_group(pieces):
        query_g, dout_g, lse_g, delta_g = pieces
        return attend_grads(query_g, dout_g, lse_g, delta_g, pooled_keys, pooled_values, scaling)

    coarse_q, coarse_k, coarse_v = lax.map(coarse_group, (grouped(queries), grouped(grad_out),
                                                          grouped_stat(coarse_lse), grouped_stat(delta_coarse)))
    pooled_key_grad = jnp.sum(coarse_k, axis=0)
    pooled_value_grad = jnp.sum(coarse_v, axis=0)
    spread_k = jnp.broadcast_to((pooled_key_grad / CUBE)[:, None], (NC, CUBE, HEADS, HEAD_DIM))
    spread_v = jnp.broadcast_to((pooled_value_grad / CUBE)[:, None], (NC, CUBE, HEADS, HEAD_DIM))
    grad_queries = (flatten(near_q) + flatten(far_q) + flatten(coarse_q)).astype(jnp.bfloat16)
    grad_keys = (flatten(near_k) + flatten(far_k) + flatten(spread_k)).astype(jnp.bfloat16)
    grad_values = (flatten(near_v) + flatten(far_v) + flatten(spread_v)).astype(jnp.bfloat16)
    return grad_queries, grad_keys, grad_values, pooled_key_grad, pooled_value_grad
```

```python
import functools

import jax
import jax.numpy as jnp
from jax import lax
from jax.experimental import pallas as pl
from jax.experimental.pallas import tpu as pltpu
from jax.sharding import PartitionSpec as P

F32 = jnp.float32
BF16 = jnp.bfloat16
VMEM_BYTES = 48 * 1024 * 1024
OFF_LSE = 1e30


def dot_nt(a, b):
    return lax.dot_general(a, b, (((1,), (1,)), ((), ())), preferred_element_type=F32)


def dot_nn(a, b):
    return lax.dot_general(a, b, (((1,), (0,)), ((), ())), preferred_element_type=F32)


def dot_tn(a, b):
    return lax.dot_general(a, b, (((0,), (0,)), ((), ())), preferred_element_type=F32)


def block_rule(q, do, lse, delta, k, v, scaling):
    probs = jnp.exp(dot_nt(k, q) * scaling - lse)
    dscores = (probs * (dot_nt(v, do) - delta)).astype(BF16)
    return probs.astype(BF16), dscores


def params(**more):
    return pltpu.CompilerParams(vmem_limit_bytes=VMEM_BYTES, **more)


def pack_kernel(splits, task_ref, q_ref, do_ref, *outs):
    for part, ref in ((0, q_ref), (1, do_ref)):
        flipped = jnp.swapaxes(ref[...].astype(F32), 0, 1).astype(BF16)
        for (low, high), out in zip(splits, outs):
            out[0, part] = flipped[low:high]


def pack(queries, grad_out, task_of_slot, cube_len, far_count, splits):
    _, heads, width = queries.shape
    slots = task_of_slot.shape[0]
    source = pl.BlockSpec((cube_len, heads, width), lambda s, t: (t[s] // far_count, 0, 0))
    sizes = [(2, high - low, cube_len, width) for low, high in splits]
    return pl.pallas_call(
        functools.partial(pack_kernel, splits),
        grid_spec=pltpu.PrefetchScalarGridSpec(
            num_scalar_prefetch=1,
            grid=(slots,),
            in_specs=[source, source],
            out_specs=[pl.BlockSpec((1,) + size, lambda s, t: (s, 0, 0, 0, 0)) for size in sizes],
        ),
        out_shape=[jax.ShapeDtypeStruct((slots,) + size, BF16) for size in sizes],
        compiler_params=params(),
    )(task_of_slot, queries, grad_out)


def near_kernel(
    scaling, chunk, q_ref, do_ref, k_ref, v_ref, pk_ref, pv_ref, stat_ref,
    dq_ref, dk_ref, dv_ref, ck_ref, cv_ref,
):
    rows = q_ref.shape[1]
    k, v, pk, pv = k_ref[0], v_ref[0], pk_ref[0], pv_ref[0]
    for start in range(0, rows, chunk):
        at = slice(start, start + chunk)
        q, do = q_ref[0, at, :], do_ref[0, at, :]
        fine = block_rule(q, do, stat_ref[0, 0:1, at], stat_ref[0, 1:2, at], k, v, scaling)
        coarse = block_rule(q, do, stat_ref[0, 2:3, at], stat_ref[0, 3:4, at], pk, pv, scaling)
        dq_ref[0, at, :] = scaling * (dot_tn(fine[1], k) + dot_tn(coarse[1], pk))
        for (probs, dscores), key_out, value_out in (
            (fine, dk_ref, dv_ref),
            (coarse, ck_ref, cv_ref),
        ):
            grad_k = scaling * dot_nn(dscores, q)
            grad_v = dot_nn(probs, do)
            if start == 0:
                key_out[0] = grad_k
                value_out[0] = grad_v
            else:
                key_out[0] += grad_k
                value_out[0] += grad_v


def near(q, do, k, v, pooled_k, pooled_v, stats, scaling):
    heads, rows, width = q.shape
    pooled = pooled_k.shape[1]
    token = pl.BlockSpec((1, rows, width), lambda h: (h, 0, 0))
    cube = pl.BlockSpec((1, pooled, width), lambda h: (h, 0, 0))
    token_out = jax.ShapeDtypeStruct((heads, rows, width), F32)
    cube_out = jax.ShapeDtypeStruct((heads, pooled, width), F32)
    return pl.pallas_call(
        functools.partial(near_kernel, scaling, min(256, rows)),
        grid=(heads,),
        in_specs=[token] * 4 + [cube] * 2 + [pl.BlockSpec((1, 4, rows), lambda h: (h, 0, 0))],
        out_specs=[token] * 3 + [cube] * 2,
        out_shape=[token_out] * 3 + [cube_out] * 2,
        compiler_params=params(),
        cost_estimate=pl.CostEstimate(
            flops=20 * heads * rows * (rows + pooled) * width,
            bytes_accessed=heads * rows * width * 20,
            transcendentals=heads * rows * (rows + pooled),
        ),
    )(q, do, k, v, pooled_k, pooled_v, stats)


def far_kernel(
    scaling, cap, asked_ref, got_ref, stat_ref, k_ref, v_ref, nk_ref, nv_ref, ok_ref, ov_ref,
    dq_ref, gk_ref, gv_ref, acc_k, acc_v,
):
    cubes, width = ok_ref.shape[1:]
    cube_len = k_ref.shape[1] // cubes
    for cube in range(cubes):
        at = slice(cube * cube_len, (cube + 1) * cube_len)
        acc_k[at, :] = nk_ref[0, at, :] + ok_ref[0, cube : cube + 1, :] * (1.0 / cube_len)
        acc_v[at, :] = nv_ref[0, at, :] + ov_ref[0, cube : cube + 1, :] * (1.0 / cube_len)
    me = lax.axis_index("seq")

    def from_source(source, carry):
        @pl.when(source != me)
        def _():
            pending = []
            for slot in range(cap):
                index = source * cap + slot
                first = pl.multiple_of(
                    jnp.maximum(asked_ref[index], 0) * cube_len, cube_len
                )
                at = pl.ds(first, cube_len)
                k, v = k_ref[0, at, :], v_ref[0, at, :]
                q, do = got_ref[index, 0, 0], got_ref[index, 1, 0]
                stat = stat_ref[0, pl.ds(index, 1), :]
                probs, dscores = block_rule(
                    q, do, stat[:, :cube_len], stat[:, cube_len:], k, v, scaling
                )
                dq_ref[index, 0] = (scaling * dot_tn(dscores, k)).astype(BF16)
                task_k = (scaling * dot_nn(dscores, q)).astype(BF16)
                task_v = dot_nn(probs, do).astype(BF16)
                pending.append((at, task_k, task_v))
            for at, task_k, task_v in pending:
                acc_k[at, :] += task_k.astype(F32)
                acc_v[at, :] += task_v.astype(F32)

        return carry

    lax.fori_loop(0, dq_ref.shape[0] // cap, from_source, 0)
    gk_ref[0] = acc_k[...].astype(BF16)
    gv_ref[0] = acc_v[...].astype(BF16)


def far(asked, got, stats, k, v, near_k, near_v, own_k, own_v, low, cap, scaling):
    slots, _, heads, cube_len, width = got.shape
    rows = k.shape[1]
    cubes = own_k.shape[1]
    token = pl.BlockSpec((1, rows, width), lambda h, a: (h + low, 0, 0))
    cube = pl.BlockSpec((1, cubes, width), lambda h, a: (h + low, 0, 0))
    out = pl.BlockSpec((1, rows, width), lambda h, a: (h, 0, 0))
    return pl.pallas_call(
        functools.partial(far_kernel, scaling, cap),
        grid_spec=pltpu.PrefetchScalarGridSpec(
            num_scalar_prefetch=1,
            grid=(heads,),
            in_specs=[
                pl.BlockSpec((slots, 2, 1, cube_len, width), lambda h, a: (0, 0, h, 0, 0)),
                pl.BlockSpec((1, slots, 2 * cube_len), lambda h, a: (h + low, 0, 0)),
                token, token, token, token, cube, cube,
            ],
            out_specs=[
                pl.BlockSpec((slots, 1, cube_len, width), lambda h, a: (0, h, 0, 0)),
                out,
                out,
            ],
            scratch_shapes=[pltpu.VMEM((rows, width), F32)] * 2,
        ),
        out_shape=[
            jax.ShapeDtypeStruct((slots, heads, cube_len, width), BF16),
            jax.ShapeDtypeStruct((heads, rows, width), BF16),
            jax.ShapeDtypeStruct((heads, rows, width), BF16),
        ],
        compiler_params=params(),
        cost_estimate=pl.CostEstimate(
            flops=100 * heads * slots * cube_len * cube_len * width,
            bytes_accessed=heads * rows * width * 30,
            transcendentals=heads * slots * cube_len * cube_len,
        ),
    )(asked, got, stats, k, v, near_k, near_v, own_k, own_v)


def join_kernel(splits, far_count, slot_ref, nq_ref, *refs):
    out = refs[-1]
    pieces = refs[:-1]
    total = []
    for part, (low, high) in enumerate(splits):
        piece = nq_ref[low:high]
        for far_at in range(far_count):
            piece = piece + pieces[part * far_count + far_at][0].astype(F32)
        total.append(piece)
    out[...] = jnp.swapaxes(jnp.concatenate(total, axis=0), 0, 1).astype(BF16)


def join(near_q, back, slot_of_task, cube_len, far_count, splits):
    heads, rows, width = near_q.shape
    specs, operands = [], []
    for (low, high), array in zip(splits, back):
        for far_at in range(far_count):
            specs.append(
                pl.BlockSpec(
                    (1, high - low, cube_len, width),
                    lambda c, s, far_at=far_at: (s[c * far_count + far_at], 0, 0, 0),
                )
            )
            operands.append(array)
    return pl.pallas_call(
        functools.partial(join_kernel, splits, far_count),
        grid_spec=pltpu.PrefetchScalarGridSpec(
            num_scalar_prefetch=1,
            grid=(rows // cube_len,),
            in_specs=[pl.BlockSpec((heads, cube_len, width), lambda c, s: (0, c, 0))] + specs,
            out_specs=pl.BlockSpec((cube_len, heads, width), lambda c, s: (c, 0, 0)),
        ),
        out_shape=jax.ShapeDtypeStruct((rows, heads, width), BF16),
        compiler_params=params(),
    )(slot_of_task, near_q, *operands)


def exchange(x):
    return lax.all_to_all(x, "seq", split_axis=0, concat_axis=0, tiled=True)


def shards(queries, keys, values, grad_out, fine_out, coarse_out, fine_lse, coarse_lse, select):
    rows, heads, width = queries.shape
    cubes, far_count = select.shape
    cube_len = rows // cubes
    scaling = width ** (-0.5)
    seq_size = lax.axis_size("seq")
    cap = max(2, min(cubes * far_count // 2, 3 * cubes * far_count // seq_size))
    slots = seq_size * cap
    tasks = cubes * far_count
    half = heads // 2
    splits = ((0, half), (half, heads))

    targets = select.reshape(-1)
    dest = targets // cubes
    local_cube = targets % cubes
    task_index = jnp.arange(tasks, dtype=jnp.int32)
    earlier = (dest[None, :] == dest[:, None]) & (task_index[None, :] < task_index[:, None])
    slot_of_task = dest * cap + jnp.sum(earlier.astype(jnp.int32), axis=1)
    matches = slot_of_task[None, :] == jnp.arange(slots, dtype=jnp.int32)[:, None]
    occupied = jnp.any(matches, axis=1)
    task_of_slot = jnp.sum(jnp.where(matches, task_index[None, :], 0), axis=1)
    cube_of_slot = jnp.where(
        occupied, jnp.sum(jnp.where(matches, local_cube[None, :], 0), axis=1), -1
    )

    sends = pack(queries, grad_out, task_of_slot, cube_len, far_count, splits)
    gots = [exchange(send.reshape((seq_size, cap) + send.shape[1:])) for send in sends]
    gots = [got.reshape((slots,) + got.shape[2:]) for got in gots]

    delta_fine = jnp.einsum("the,the->ht", grad_out, fine_out, preferred_element_type=F32)
    delta_coarse = jnp.einsum("the,the->ht", grad_out, coarse_out, preferred_element_type=F32)

    def task_stat(x):
        return x.reshape(heads, cubes, cube_len).transpose(1, 0, 2)[task_of_slot // far_count]

    slot_lse = jnp.where(occupied[:, None, None], task_stat(fine_lse), OFF_LSE)
    slot_stats = jnp.concatenate([slot_lse, task_stat(delta_fine)], axis=2)
    got_stats = exchange(slot_stats.reshape(seq_size, cap, heads, 2 * cube_len))
    got_stats = got_stats.reshape(slots, heads, 2 * cube_len).transpose(1, 0, 2)
    asked = exchange(cube_of_slot.reshape(seq_size, cap)).reshape(-1)

    def pooled(x):
        mean = jnp.mean(x.reshape(cubes, cube_len, heads, width), axis=1, dtype=F32)
        return mean.astype(BF16).transpose(1, 0, 2)

    all_pooled = lax.all_gather(
        jnp.concatenate([pooled(keys), pooled(values)], axis=0), "seq", axis=1, tiled=True
    )
    q, do, k, v = (x.transpose(1, 0, 2) for x in (queries, grad_out, keys, values))
    stats = jnp.stack([fine_lse, delta_fine, coarse_lse, delta_coarse], axis=1)
    near_q, near_k, near_v, coarse_k, coarse_v = near(
        q, do, k, v, all_pooled[:heads], all_pooled[heads:], stats, scaling
    )
    own = lax.psum_scatter(
        jnp.concatenate([coarse_k, coarse_v], axis=0), "seq", scatter_dimension=1, tiled=True
    )
    own_k, own_v = own[:heads], own[heads:]

    back, grads_k, grads_v = [], [], []
    for (low, high), got in zip(splits, gots):
        task_q, grad_k, grad_v = far(
            asked, got, got_stats, k, v, near_k, near_v, own_k, own_v, low, cap, scaling
        )
        returned = exchange(task_q.reshape((seq_size, cap) + task_q.shape[1:]))
        back.append(returned.reshape(task_q.shape))
        grads_k.append(grad_k)
        grads_v.append(grad_v)
    grad_queries = join(near_q, back, slot_of_task, cube_len, far_count, splits)
    grad_keys = jnp.concatenate(grads_k, axis=0).transpose(1, 0, 2)
    grad_values = jnp.concatenate(grads_v, axis=0).transpose(1, 0, 2)
    return (
        grad_queries,
        grad_keys,
        grad_values,
        own_k.transpose(1, 0, 2),
        own_v.transpose(1, 0, 2),
    )


def solution(mesh):
    token = P(("groups", "seq"), ("head", "pair"), None)
    stat = P(("head", "pair"), ("groups", "seq"))
    return jax.shard_map(
        shards,
        mesh=mesh,
        in_specs=(token,) * 6 + (stat, stat, P(("groups", "seq"), None)),
        out_specs=(token,) * 5,
        check_vma=False,
    )
```

```python
import functools

import jax
import jax.numpy as jnp
from jax import lax
from jax.experimental import pallas as pl
from jax.experimental.pallas import tpu as pltpu
from jax.sharding import PartitionSpec as P

F32 = jnp.float32
BF16 = jnp.bfloat16
VMEM_BYTES = 48 * 1024 * 1024
OFF_LSE = 1e30


def dot_nt(a, b):
    return lax.dot_general(a, b, (((1,), (1,)), ((), ())), preferred_element_type=F32)


def dot_nn(a, b):
    return lax.dot_general(a, b, (((1,), (0,)), ((), ())), preferred_element_type=F32)


def dot_tn(a, b):
    return lax.dot_general(a, b, (((0,), (0,)), ((), ())), preferred_element_type=F32)


def block_rule(q, do, lse, delta, k, v, scaling):
    probs = jnp.exp(dot_nt(k, q) * scaling - lse)
    dscores = (probs * (dot_nt(v, do) - delta)).astype(BF16)
    return probs.astype(BF16), dscores


def params(**more):
    return pltpu.CompilerParams(vmem_limit_bytes=VMEM_BYTES, **more)


def pack_kernel(splits, task_ref, q_ref, do_ref, *outs):
    for part, ref in ((0, q_ref), (1, do_ref)):
        flipped = jnp.swapaxes(ref[...].astype(F32), 0, 1).astype(BF16)
        for (low, high), out in zip(splits, outs):
            out[0, part] = flipped[low:high]


def pack(queries, grad_out, task_of_slot, cube_len, far_count, splits):
    _, heads, width = queries.shape
    slots = task_of_slot.shape[0]
    source = pl.BlockSpec((cube_len, heads, width), lambda s, t: (t[s] // far_count, 0, 0))
    sizes = [(2, high - low, cube_len, width) for low, high in splits]
    return pl.pallas_call(
        functools.partial(pack_kernel, splits),
        grid_spec=pltpu.PrefetchScalarGridSpec(
            num_scalar_prefetch=1,
            grid=(slots,),
            in_specs=[source, source],
            out_specs=[pl.BlockSpec((1,) + size, lambda s, t: (s, 0, 0, 0, 0)) for size in sizes],
        ),
        out_shape=[jax.ShapeDtypeStruct((slots,) + size, BF16) for size in sizes],
        compiler_params=params(),
    )(task_of_slot, queries, grad_out)


def near_kernel(
    scaling, chunk, q_ref, do_ref, k_ref, v_ref, pk_ref, pv_ref, stat_ref,
    dq_ref, dk_ref, dv_ref, ck_ref, cv_ref,
):
    rows = q_ref.shape[1]
    k, v, pk, pv = k_ref[0], v_ref[0], pk_ref[0], pv_ref[0]
    for start in range(0, rows, chunk):
        at = slice(start, start + chunk)
        q, do = q_ref[0, at, :], do_ref[0, at, :]
        fine = block_rule(q, do, stat_ref[0, 0:1, at], stat_ref[0, 1:2, at], k, v, scaling)
        coarse = block_rule(q, do, stat_ref[0, 2:3, at], stat_ref[0, 3:4, at], pk, pv, scaling)
        dq_ref[0, at, :] = scaling * (dot_tn(fine[1], k) + dot_tn(coarse[1], pk))
        for (probs, dscores), key_out, value_out in (
            (fine, dk_ref, dv_ref),
            (coarse, ck_ref, cv_ref),
        ):
            grad_k = scaling * dot_nn(dscores, q)
            grad_v = dot_nn(probs, do)
            if start == 0:
                key_out[0] = grad_k
                value_out[0] = grad_v
            else:
                key_out[0] += grad_k
                value_out[0] += grad_v


def near(q, do, k, v, pooled_k, pooled_v, stats, scaling):
    heads, rows, width = q.shape
    pooled = pooled_k.shape[1]
    token = pl.BlockSpec((1, rows, width), lambda h: (h, 0, 0))
    cube = pl.BlockSpec((1, pooled, width), lambda h: (h, 0, 0))
    token_out = jax.ShapeDtypeStruct((heads, rows, width), F32)
    cube_out = jax.ShapeDtypeStruct((heads, pooled, width), F32)
    return pl.pallas_call(
        functools.partial(near_kernel, scaling, min(256, rows)),
        grid=(heads,),
        in_specs=[token] * 4 + [cube] * 2 + [pl.BlockSpec((1, 4, rows), lambda h: (h, 0, 0))],
        out_specs=[token] * 3 + [cube] * 2,
        out_shape=[token_out] * 3 + [cube_out] * 2,
        compiler_params=params(),
        cost_estimate=pl.CostEstimate(
            flops=20 * heads * rows * (rows + pooled) * width,
            bytes_accessed=heads * rows * width * 20,
            transcendentals=heads * rows * (rows + pooled),
        ),
    )(q, do, k, v, pooled_k, pooled_v, stats)


def far_kernel(scaling, cap, steps, asked_ref, *refs):
    gots = refs[:steps]
    stat_ref, k_ref, v_ref, nk_ref, nv_ref, ok_ref, ov_ref = refs[steps : steps + 7]
    dqs = refs[steps + 7 : 2 * steps + 7]
    gk_ref, gv_ref, acc_k, acc_v = refs[2 * steps + 7 :]
    cubes, width = ok_ref.shape[1:]
    cube_len = k_ref.shape[1] // cubes
    for cube in range(cubes):
        at = slice(cube * cube_len, (cube + 1) * cube_len)
        acc_k[at, :] = nk_ref[0, at, :] + ok_ref[0, cube : cube + 1, :] * (1.0 / cube_len)
        acc_v[at, :] = nv_ref[0, at, :] + ov_ref[0, cube : cube + 1, :] * (1.0 / cube_len)
    for step in range(steps):
        pending = []
        for slot in range(cap):
            index = step * cap + slot
            first = pl.multiple_of(asked_ref[index] * cube_len, cube_len)
            at = pl.ds(first, cube_len)
            k, v = k_ref[0, at, :], v_ref[0, at, :]
            q, do = gots[step][slot, 0, 0], gots[step][slot, 1, 0]
            stat = stat_ref[0, index : index + 1, :]
            probs, dscores = block_rule(
                q, do, stat[:, :cube_len], stat[:, cube_len:], k, v, scaling
            )
            dqs[step][slot, 0] = (scaling * dot_tn(dscores, k)).astype(BF16)
            task_k = (scaling * dot_nn(dscores, q)).astype(BF16)
            task_v = dot_nn(probs, do).astype(BF16)
            pending.append((at, task_k, task_v))
        for at, task_k, task_v in pending:
            acc_k[at, :] += task_k.astype(F32)
            acc_v[at, :] += task_v.astype(F32)
    gk_ref[0] = acc_k[...].astype(BF16)
    gv_ref[0] = acc_v[...].astype(BF16)


def far(asked, gots, stats, k, v, near_k, near_v, own_k, own_v, low, scaling):
    steps = len(gots)
    cap, _, heads, cube_len, width = gots[0].shape
    slots = steps * cap
    rows = k.shape[1]
    cubes = own_k.shape[1]
    token = pl.BlockSpec((1, rows, width), lambda h, a: (h + low, 0, 0))
    cube = pl.BlockSpec((1, cubes, width), lambda h, a: (h + low, 0, 0))
    out = pl.BlockSpec((1, rows, width), lambda h, a: (h, 0, 0))
    got = pl.BlockSpec((cap, 2, 1, cube_len, width), lambda h, a: (0, 0, h, 0, 0))
    dq = pl.BlockSpec((cap, 1, cube_len, width), lambda h, a: (0, h, 0, 0))
    results = pl.pallas_call(
        functools.partial(far_kernel, scaling, cap, steps),
        grid_spec=pltpu.PrefetchScalarGridSpec(
            num_scalar_prefetch=1,
            grid=(heads,),
            in_specs=[got] * steps
            + [pl.BlockSpec((1, slots, 2 * cube_len), lambda h, a: (h + low, 0, 0))]
            + [token] * 4
            + [cube] * 2,
            out_specs=[dq] * steps + [out] * 2,
            scratch_shapes=[pltpu.VMEM((rows, width), F32)] * 2,
        ),
        out_shape=[jax.ShapeDtypeStruct((cap, heads, cube_len, width), BF16)] * steps
        + [jax.ShapeDtypeStruct((heads, rows, width), BF16)] * 2,
        compiler_params=params(),
        cost_estimate=pl.CostEstimate(
            flops=100 * heads * slots * cube_len * cube_len * width,
            bytes_accessed=heads * rows * width * 30,
            transcendentals=heads * slots * cube_len * cube_len,
        ),
    )(asked, *gots, stats, k, v, near_k, near_v, own_k, own_v)
    return results[:steps], results[steps], results[steps + 1]


def join_kernel(splits, steps, cap, far_count, slot_ref, nq_ref, *refs):
    out = refs[-1]
    pieces = iter(refs[:-1])
    cube = pl.program_id(0)
    total = []
    for low, high in splits:
        piece = nq_ref[low:high]
        for step in range(steps):
            for far_at in range(far_count):
                slot = slot_ref[cube * far_count + far_at]
                here = (slot >= step * cap) & (slot < (step + 1) * cap)
                piece = piece + jnp.where(here, next(pieces)[0].astype(F32), 0.0)
        total.append(piece)
    out[...] = jnp.swapaxes(jnp.concatenate(total, axis=0), 0, 1).astype(BF16)


def join(near_q, back, slot_of_task, cube_len, far_count, splits):
    heads, rows, width = near_q.shape
    steps, cap = len(back[0]), back[0][0].shape[0]
    specs, operands = [], []
    for (low, high), arrays in zip(splits, back):
        for step in range(steps):
            for far_at in range(far_count):

                def place(c, s, step=step, far_at=far_at):
                    slot = s[c * far_count + far_at] - step * cap
                    return (jnp.clip(slot, 0, cap - 1), 0, 0, 0)

                specs.append(pl.BlockSpec((1, high - low, cube_len, width), place))
                operands.append(arrays[step])
    return pl.pallas_call(
        functools.partial(join_kernel, splits, steps, cap, far_count),
        grid_spec=pltpu.PrefetchScalarGridSpec(
            num_scalar_prefetch=1,
            grid=(rows // cube_len,),
            in_specs=[pl.BlockSpec((heads, cube_len, width), lambda c, s: (0, c, 0))] + specs,
            out_specs=pl.BlockSpec((cube_len, heads, width), lambda c, s: (c, 0, 0)),
        ),
        out_shape=jax.ShapeDtypeStruct((rows, heads, width), BF16),
        compiler_params=params(),
    )(slot_of_task, near_q, *operands)


def shift(x, step):
    size = lax.axis_size("seq")
    return lax.ppermute(x, "seq", [(i, (i + step) % size) for i in range(size)])


def shards(queries, keys, values, grad_out, fine_out, coarse_out, fine_lse, coarse_lse, select):
    rows, heads, width = queries.shape
    cubes, far_count = select.shape
    cube_len = rows // cubes
    scaling = width ** (-0.5)
    seq_size = lax.axis_size("seq")
    cap = max(2, min(cubes * far_count // 2, 3 * cubes * far_count // seq_size))
    steps = seq_size - 1
    slots = steps * cap
    tasks = cubes * far_count
    half = heads // 2
    splits = ((0, half), (half, heads))
    me = lax.axis_index("seq")

    targets = select.reshape(-1)
    away = (targets // cubes - me + seq_size) % seq_size
    local_cube = targets % cubes
    task_index = jnp.arange(tasks, dtype=jnp.int32)
    earlier = (away[None, :] == away[:, None]) & (task_index[None, :] < task_index[:, None])
    slot_of_task = (away - 1) * cap + jnp.sum(earlier.astype(jnp.int32), axis=1)
    matches = slot_of_task[None, :] == jnp.arange(slots, dtype=jnp.int32)[:, None]
    occupied = jnp.any(matches, axis=1)
    task_of_slot = jnp.sum(jnp.where(matches, task_index[None, :], 0), axis=1)
    cube_of_slot = jnp.sum(jnp.where(matches, local_cube[None, :], 0), axis=1)

    def of_step(x, step):
        return x[step * cap : (step + 1) * cap]

    sends = [
        pack(queries, grad_out, of_step(task_of_slot, s), cube_len, far_count, splits)
        for s in range(steps)
    ]
    first = [shift(sends[s][0], s + 1) for s in range(steps)]

    def pooled(x):
        mean = jnp.mean(x.reshape(cubes, cube_len, heads, width), axis=1, dtype=F32)
        return mean.astype(BF16).transpose(1, 0, 2)

    own_pooled = jnp.concatenate([pooled(keys), pooled(values)], axis=0)
    all_pooled = jnp.concatenate(
        [own_pooled] + [shift(own_pooled, -s) for s in range(1, seq_size)], axis=1
    )

    delta_fine = jnp.einsum("the,the->ht", grad_out, fine_out, preferred_element_type=F32)
    delta_coarse = jnp.einsum("the,the->ht", grad_out, coarse_out, preferred_element_type=F32)

    def task_stat(x):
        return x.reshape(heads, cubes, cube_len).transpose(1, 0, 2)[task_of_slot // far_count]

    slot_lse = jnp.where(occupied[:, None, None], task_stat(fine_lse), OFF_LSE)
    slot_stats = jnp.concatenate([slot_lse, task_stat(delta_fine)], axis=2)
    slot_cube = jnp.broadcast_to(
        cube_of_slot.astype(F32)[:, None, None], (slots, 1, 2 * cube_len)
    )
    slot_stats = jnp.concatenate([slot_stats, slot_cube], axis=1)
    got_stats = jnp.concatenate([shift(of_step(slot_stats, s), s + 1) for s in range(steps)], axis=0)
    asked = got_stats[:, heads, 0].astype(jnp.int32)
    got_stats = got_stats[:, :heads].transpose(1, 0, 2)

    q, do, k, v = (x.transpose(1, 0, 2) for x in (queries, grad_out, keys, values))
    stats = jnp.stack([fine_lse, delta_fine, coarse_lse, delta_coarse], axis=1)
    near_q, near_k, near_v, coarse_k, coarse_v = near(
        q, do, k, v, all_pooled[:heads], all_pooled[heads:], stats, scaling
    )

    coarse = jnp.concatenate([coarse_k, coarse_v], axis=0)
    own = coarse[:, :cubes]
    for s in range(1, seq_size):
        own = own + shift(coarse[:, s * cubes : (s + 1) * cubes], s)
    own_k, own_v = own[:heads], own[heads:]

    later = [send[1] for send in sends]
    first, later = lax.optimization_barrier((first, later))
    second = [shift(later[s], s + 1) for s in range(steps)]

    back, grads_k, grads_v = [], [], []
    for (low, high), gots in zip(splits, (first, second)):
        task_q, grad_k, grad_v = far(
            asked, gots, got_stats, k, v, near_k, near_v, own_k, own_v, low, scaling
        )
        back.append([shift(task_q[s], -(s + 1)) for s in range(steps)])
        grads_k.append(grad_k)
        grads_v.append(grad_v)
    grad_queries = join(near_q, back, slot_of_task, cube_len, far_count, splits)
    grad_keys = jnp.concatenate(grads_k, axis=0).transpose(1, 0, 2)
    grad_values = jnp.concatenate(grads_v, axis=0).transpose(1, 0, 2)
    return (
        grad_queries,
        grad_keys,
        grad_values,
        own_k.transpose(1, 0, 2),
        own_v.transpose(1, 0, 2),
    )


def solution(mesh):
    token = P(("groups", "seq"), ("head", "pair"), None)
    stat = P(("head", "pair"), ("groups", "seq"))
    return jax.shard_map(
        shards,
        mesh=mesh,
        in_specs=(token,) * 6 + (stat, stat, P(("groups", "seq"), None)),
        out_specs=(token,) * 5,
        check_vma=False,
    )
```

```python
import functools

import jax
import jax.numpy as jnp
from jax import lax
from jax.experimental import pallas as pl
from jax.experimental.pallas import tpu as pltpu
from jax.sharding import PartitionSpec as P

F32 = jnp.float32
BF16 = jnp.bfloat16
VMEM_BYTES = 48 * 1024 * 1024
OFF_LSE = 1e30


def dot_nt(a, b):
    return lax.dot_general(a, b, (((1,), (1,)), ((), ())), preferred_element_type=F32)


def dot_nn(a, b):
    return lax.dot_general(a, b, (((1,), (0,)), ((), ())), preferred_element_type=F32)


def dot_tn(a, b):
    return lax.dot_general(a, b, (((0,), (0,)), ((), ())), preferred_element_type=F32)


def block_rule(q, do, lse, delta, k, v, scaling):
    probs = jnp.exp(dot_nt(k, q) * scaling - lse)
    dscores = (probs * (dot_nt(v, do) - delta)).astype(BF16)
    return probs.astype(BF16), dscores


def params(**more):
    return pltpu.CompilerParams(vmem_limit_bytes=VMEM_BYTES, **more)


def pack_kernel(steps, task_ref, *refs):
    for step in range(steps):
        refs[2 * steps + step][0, 0] = refs[step][...]
        refs[2 * steps + step][0, 1] = refs[steps + step][...]


def pack(q, do, task_of_slot, cube_len, far_count, steps, split):
    low, high = split
    heads, width = high - low, q.shape[2]
    cap = task_of_slot.shape[0] // steps
    block = low // heads
    if low % heads:
        q, do, block = q[low:high], do[low:high], 0

    def source(step):
        return pl.BlockSpec(
            (heads, cube_len, width),
            lambda s, t: (block, t[step * cap + s] // far_count, 0),
        )

    size = (2, heads, cube_len, width)
    return pl.pallas_call(
        functools.partial(pack_kernel, steps),
        grid_spec=pltpu.PrefetchScalarGridSpec(
            num_scalar_prefetch=1,
            grid=(cap,),
            in_specs=[source(step) for step in range(steps)] * 2,
            out_specs=[pl.BlockSpec((1,) + size, lambda s, t: (s, 0, 0, 0, 0))] * steps,
        ),
        out_shape=[jax.ShapeDtypeStruct((cap,) + size, BF16)] * steps,
        compiler_params=params(),
    )(task_of_slot, *([q] * steps), *([do] * steps))


def near_kernel(
    scaling, chunk, q_ref, do_ref, k_ref, v_ref, pk_ref, pv_ref, stat_ref,
    dq_ref, dk_ref, dv_ref, ck_ref, cv_ref,
):
    rows = q_ref.shape[1]
    k, v, pk, pv = k_ref[0], v_ref[0], pk_ref[0], pv_ref[0]
    for start in range(0, rows, chunk):
        at = slice(start, start + chunk)
        q, do = q_ref[0, at, :], do_ref[0, at, :]
        fine = block_rule(q, do, stat_ref[0, 0:1, at], stat_ref[0, 1:2, at], k, v, scaling)
        coarse = block_rule(q, do, stat_ref[0, 2:3, at], stat_ref[0, 3:4, at], pk, pv, scaling)
        dq_ref[0, at, :] = scaling * (dot_tn(fine[1], k) + dot_tn(coarse[1], pk))
        for (probs, dscores), key_out, value_out in (
            (fine, dk_ref, dv_ref),
            (coarse, ck_ref, cv_ref),
        ):
            grad_k = scaling * dot_nn(dscores, q)
            grad_v = dot_nn(probs, do)
            if start == 0:
                key_out[0] = grad_k
                value_out[0] = grad_v
            else:
                key_out[0] += grad_k
                value_out[0] += grad_v


def near(q, do, k, v, pooled_k, pooled_v, stats, scaling):
    heads, rows, width = q.shape
    pooled = pooled_k.shape[1]
    token = pl.BlockSpec((1, rows, width), lambda h: (h, 0, 0))
    cube = pl.BlockSpec((1, pooled, width), lambda h: (h, 0, 0))
    token_out = jax.ShapeDtypeStruct((heads, rows, width), F32)
    cube_out = jax.ShapeDtypeStruct((heads, pooled, width), F32)
    return pl.pallas_call(
        functools.partial(near_kernel, scaling, min(256, rows)),
        grid=(heads,),
        in_specs=[token] * 4 + [cube] * 2 + [pl.BlockSpec((1, 4, rows), lambda h: (h, 0, 0))],
        out_specs=[token] * 3 + [cube] * 2,
        out_shape=[token_out] * 3 + [cube_out] * 2,
        compiler_params=params(),
        cost_estimate=pl.CostEstimate(
            flops=20 * heads * rows * (rows + pooled) * width,
            bytes_accessed=heads * rows * width * 20,
            transcendentals=heads * rows * (rows + pooled),
        ),
    )(q, do, k, v, pooled_k, pooled_v, stats)


def far_kernel(scaling, cap, steps, asked_ref, *refs):
    gots = refs[:steps]
    stat_ref, k_ref, v_ref, nk_ref, nv_ref = refs[steps : steps + 5]
    dqs = refs[steps + 6 : 2 * steps + 6]
    acc_k, acc_v = refs[2 * steps + 6 :]
    cube_len = gots[0].shape[3]
    acc_k[...] = nk_ref[...]
    acc_v[...] = nv_ref[...]
    for step in range(steps):
        pending = []
        for slot in range(cap):
            index = step * cap + slot
            first = pl.multiple_of(asked_ref[index] * cube_len, cube_len)
            at = pl.ds(first, cube_len)
            k, v = k_ref[0, at, :], v_ref[0, at, :]
            q, do = gots[step][slot, 0, 0], gots[step][slot, 1, 0]
            stat = stat_ref[0, index : index + 1, :]
            probs, dscores = block_rule(
                q, do, stat[:, :cube_len], stat[:, cube_len:], k, v, scaling
            )
            dqs[step][slot, 0] = (scaling * dot_tn(dscores, k)).astype(BF16)
            task_k = (scaling * dot_nn(dscores, q)).astype(BF16)
            task_v = dot_nn(probs, do).astype(BF16)
            pending.append((at, task_k, task_v))
        for at, task_k, task_v in pending:
            acc_k[0, at, :] += task_k.astype(F32)
            acc_v[0, at, :] += task_v.astype(F32)


def far(asked, gots, stats, k, v, near_k, near_v, after, low, scaling):
    steps = len(gots)
    cap, _, heads, cube_len, width = gots[0].shape
    slots = steps * cap
    rows = k.shape[1]
    token = pl.BlockSpec((1, rows, width), lambda h, a: (h + low, 0, 0))
    out = pl.BlockSpec((1, rows, width), lambda h, a: (h, 0, 0))
    got = pl.BlockSpec((cap, 2, 1, cube_len, width), lambda h, a: (0, 0, h, 0, 0))
    dq = pl.BlockSpec((cap, 1, cube_len, width), lambda h, a: (0, h, 0, 0))
    results = pl.pallas_call(
        functools.partial(far_kernel, scaling, cap, steps),
        grid_spec=pltpu.PrefetchScalarGridSpec(
            num_scalar_prefetch=1,
            grid=(heads,),
            in_specs=[got] * steps
            + [pl.BlockSpec((1, slots, 2 * cube_len), lambda h, a: (h + low, 0, 0))]
            + [token] * 4
            + [pl.BlockSpec(memory_space=pl.ANY)],
            out_specs=[dq] * steps + [out] * 2,
        ),
        out_shape=[jax.ShapeDtypeStruct((cap, heads, cube_len, width), BF16)] * steps
        + [jax.ShapeDtypeStruct((heads, rows, width), F32)] * 2,
        compiler_params=params(),
        cost_estimate=pl.CostEstimate(
            flops=100 * heads * slots * cube_len * cube_len * width,
            bytes_accessed=heads * rows * width * 30,
            transcendentals=heads * slots * cube_len * cube_len,
        ),
    )(asked, *gots, stats, k, v, near_k, near_v, after)
    return results[:steps], results[steps], results[steps + 1]


def join_kernel(splits, steps, cap, far_count, slot_ref, nq_ref, *refs):
    out = refs[-1]
    pieces = iter(refs[:-1])
    cube = pl.program_id(0)
    for low, high in splits:
        piece = nq_ref[low:high]
        for step in range(steps):
            for far_at in range(far_count):
                slot = slot_ref[cube * far_count + far_at]
                here = (slot >= step * cap) & (slot < (step + 1) * cap)
                piece = piece + jnp.where(here, next(pieces)[0].astype(F32), 0.0)
        out[low:high] = piece.astype(BF16)


def join(near_q, back, slot_of_task, cube_len, far_count, splits):
    heads, rows, width = near_q.shape
    steps, cap = len(back[0]), back[0][0].shape[0]
    specs, operands = [], []
    for (low, high), arrays in zip(splits, back):
        for step in range(steps):
            for far_at in range(far_count):

                def place(c, s, step=step, far_at=far_at):
                    slot = s[c * far_count + far_at] - step * cap
                    return (jnp.clip(slot, 0, cap - 1), 0, 0, 0)

                specs.append(pl.BlockSpec((1, high - low, cube_len, width), place))
                operands.append(arrays[step])
    return pl.pallas_call(
        functools.partial(join_kernel, splits, steps, cap, far_count),
        grid_spec=pltpu.PrefetchScalarGridSpec(
            num_scalar_prefetch=1,
            grid=(rows // cube_len,),
            in_specs=[pl.BlockSpec((heads, cube_len, width), lambda c, s: (0, c, 0))] + specs,
            out_specs=pl.BlockSpec((heads, cube_len, width), lambda c, s: (0, c, 0)),
        ),
        out_shape=jax.ShapeDtypeStruct((heads, rows, width), BF16),
        compiler_params=params(),
    )(slot_of_task, near_q, *operands)


def shift(x, step):
    size = lax.axis_size("seq")
    return lax.ppermute(x, "seq", [(i, (i + step) % size) for i in range(size)])


def shards(queries, keys, values, grad_out, fine_out, coarse_out, fine_lse, coarse_lse, select):
    rows, heads, width = queries.shape
    cubes, far_count = select.shape
    cube_len = rows // cubes
    scaling = width ** (-0.5)
    seq_size = lax.axis_size("seq")
    cap = max(2, min(cubes * far_count // 2, 3 * cubes * far_count // seq_size))
    steps = seq_size - 1
    slots = steps * cap
    tasks = cubes * far_count
    half = heads // 2
    splits = ((0, half), (half, heads))
    me = lax.axis_index("seq")

    targets = select.reshape(-1)
    away = (targets // cubes - me + seq_size) % seq_size
    local_cube = targets % cubes
    task_index = jnp.arange(tasks, dtype=jnp.int32)
    earlier = (away[None, :] == away[:, None]) & (task_index[None, :] < task_index[:, None])
    slot_of_task = (away - 1) * cap + jnp.sum(earlier.astype(jnp.int32), axis=1)
    matches = slot_of_task[None, :] == jnp.arange(slots, dtype=jnp.int32)[:, None]
    occupied = jnp.any(matches, axis=1)
    task_of_slot = jnp.sum(jnp.where(matches, task_index[None, :], 0), axis=1)
    cube_of_slot = jnp.sum(jnp.where(matches, local_cube[None, :], 0), axis=1)

    def of_step(x, step):
        return x[step * cap : (step + 1) * cap]

    def pack_half(split):
        return pack(q, do, task_of_slot, cube_len, far_count, steps, split)

    q, do = queries.transpose(1, 0, 2), grad_out.transpose(1, 0, 2)
    sends = pack_half(splits[0])
    sends, keys, values, fine_out, coarse_out, grad_out, q, do = lax.optimization_barrier(
        (sends, keys, values, fine_out, coarse_out, grad_out, q, do)
    )
    first = [shift(sends[s], s + 1) for s in range(steps)]
    later = pack_half(splits[1])

    def pooled(x):
        mean = jnp.mean(x.reshape(cubes, cube_len, heads, width), axis=1, dtype=F32)
        return mean.astype(BF16).transpose(1, 0, 2)

    own_pooled = jnp.concatenate([pooled(keys), pooled(values)], axis=0)
    all_pooled = jnp.concatenate(
        [own_pooled] + [shift(own_pooled, -s) for s in range(1, seq_size)], axis=1
    )

    delta_fine = jnp.einsum("the,the->ht", grad_out, fine_out, preferred_element_type=F32)
    delta_coarse = jnp.einsum("the,the->ht", grad_out, coarse_out, preferred_element_type=F32)

    def task_stat(x):
        return x.reshape(heads, cubes, cube_len).transpose(1, 0, 2)[task_of_slot // far_count]

    slot_lse = jnp.where(occupied[:, None, None], task_stat(fine_lse), OFF_LSE)
    slot_stats = jnp.concatenate([slot_lse, task_stat(delta_fine)], axis=2)
    slot_cube = jnp.broadcast_to(
        cube_of_slot.astype(F32)[:, None, None], (slots, 1, 2 * cube_len)
    )
    slot_stats = jnp.concatenate([slot_stats, slot_cube], axis=1)
    got_stats = jnp.concatenate([shift(of_step(slot_stats, s), s + 1) for s in range(steps)], axis=0)
    asked = got_stats[:, heads, 0].astype(jnp.int32)
    got_stats = got_stats[:, :heads].transpose(1, 0, 2)

    k, v = keys.transpose(1, 0, 2), values.transpose(1, 0, 2)
    stats = jnp.stack([fine_lse, delta_fine, coarse_lse, delta_coarse], axis=1)
    near_q, near_k, near_v, coarse_k, coarse_v = near(
        q, do, k, v, all_pooled[:heads], all_pooled[heads:], stats, scaling
    )

    coarse = jnp.concatenate([coarse_k, coarse_v], axis=0)
    own = coarse[:, :cubes]
    for s in range(1, seq_size):
        piece = coarse[:, s * cubes : (s + 1) * cubes].astype(BF16)
        own = own + shift(piece, s).astype(F32)

    first, later, near_q, near_k, near_v = lax.optimization_barrier(
        (first, later, near_q, near_k, near_v)
    )
    second = [shift(later[s], s + 1) for s in range(steps)]

    def far_half(split, gots, after):
        return far(asked, gots, got_stats, k, v, near_k, near_v, after, split[0], scaling)

    def give_back(task_q):
        return [shift(task_q[s], -(s + 1)) for s in range(steps)]

    task_q, sum_k, sum_v = far_half(splits[0], first, first[0][0, 0, 0, :16])
    task_q, second = lax.optimization_barrier((task_q, second))
    back = [give_back(task_q)]
    mark = shift(task_q[-1][0, 0, :16], 1)
    sums_k, sums_v = [sum_k], [sum_v]
    task_q, sum_k, sum_v = far_half(splits[1], second, mark)
    back.append(give_back(task_q))
    sums_k.append(sum_k)
    sums_v.append(sum_v)

    def with_pooled(sums, pooled_grad):
        parts = []
        for (low, high), part in zip(splits, sums):
            spread = (pooled_grad[low:high] / cube_len)[:, :, None, :]
            part = part.reshape(high - low, cubes, cube_len, width) + spread
            parts.append(part.astype(BF16).reshape(high - low, rows, width))
        return jnp.concatenate(parts, axis=0).transpose(1, 0, 2)

    own_k, own_v = own[:heads], own[heads:]
    grad_keys = with_pooled(sums_k, own_k)
    grad_values = with_pooled(sums_v, own_v)
    grad_queries = join(near_q, back, slot_of_task, cube_len, far_count, splits)
    grad_queries = grad_queries.transpose(1, 0, 2)
    return (
        grad_queries,
        grad_keys,
        grad_values,
        own_k.transpose(1, 0, 2),
        own_v.transpose(1, 0, 2),
    )


def solution(mesh):
    token = P(("groups", "seq"), ("head", "pair"), None)
    stat = P(("head", "pair"), ("groups", "seq"))
    return jax.shard_map(
        shards,
        mesh=mesh,
        in_specs=(token,) * 6 + (stat, stat, P(("groups", "seq"), None)),
        out_specs=(token,) * 5,
        check_vma=False,
    )
```
